256 devices in a mesh: section: 16 (over z_hi, x, core), tp: 16 (over y, z_lo).
Axes of the slice: x: 4, y: 4, z: 8 (z_hi: 2, z_lo: 4; z = z_hi * 4 + z_lo), core: 2. Of those that a mesh axis runs over, the one named last changes fastest.
Arguments:
- query: bfloat16 [16, 2, 1024, 4096], P('section', None, 'tp'), may hold values from -6 to 6
- keys_values: bfloat16 [16, 2, 2, 1024, 512], P('section', None, None, 'tp'), may hold values from -6 to 6
- grad_out: bfloat16 [16, 2, 1024, 4096], P('section', None, 'tp'), may hold values from -6 to 6
- fwd_query: bfloat16 [16, 2, 1024, 4096], P('section', None, 'tp'), may hold values from -6 to 6
- fwd_keys_values: bfloat16 [16, 2, 2, 1024, 512], P('section', None, None, 'tp'), may hold values from -6 to 6
- held_out: bfloat16 [16, 2, 1024, 4096], P('section', None, None, 'tp'), may hold values from -4 to 4
- evict: int32 [8, 2, 2], replicated, may hold values from 0 to 1
Outputs:
- passed_on: bfloat16 [16, 2, 1024, 4096], P('section', None, 'tp')
- grad_query: bfloat16 [16, 2, 1024, 4096], P('section', None, 'tp')
- grad_keys_values: bfloat16 [16, 2, 2, 1024, 512], P('section', None, None, 'tp')
- mirror_out: bfloat16 [16, 2, 1024, 4096], P('section', None, None, 'tp')
The draws below stay inside these ranges and needn't reach their ends.
All inputs are finite; a program needn't handle non-finite values.
Results may differ from the reference program's by a relative error of at most 0.0057.
Values may be sent and summed in bfloat16 or wider, within the bound.
No kernel may reach another device: no remote copies, remote signals or barrier semaphores. Data moves between devices by JAX's collectives and lax.ppermute only.
A program may use at most 128 MiB of HBM per device.

```python
import math
import jax
import jax.numpy as jnp
from jax import lax

HEADS = 32
KV_HEADS = 4
HD = 128
SEQ = 1024
MB = 2
N_SECTION = 16


def touch_ends(result, own_key, smallest, high):
    extent = result.shape
    index_at = [jax.random.randint(jax.random.fold_in(own_key, axis), (), 0, extent[axis]) for axis in range(len(extent))]
    result = result.at[tuple(index_at)].set(smallest)
    longest = extent.index(max(extent))
    index_at[longest] = (index_at[longest] + 1) % extent[longest]
    return result.at[tuple(index_at)].set(high)


def levels(own_key, dims, split, smallest, largest):
    loudness = 1.0
    for axis_at, shards_of in split:
        heights = jax.random.uniform(jax.random.fold_in(jax.random.fold_in(own_key, 6), axis_at), (shards_of,), jnp.float32, smallest / len(split), largest / len(split))
        loudness = loudness * jnp.repeat(jnp.exp(heights), dims[axis_at] // shards_of).reshape((-1,) + (1,) * (len(dims) - 1 - axis_at))
    return loudness


def centred(stream_key, dims, spread, limit, pieces=(), held_as=jnp.bfloat16):
    gain = levels(stream_key, dims, pieces, -0.22, 0.18) if pieces else 1.0
    drawn = jax.random.normal(stream_key, dims, jnp.float32) * spread * gain
    return jnp.minimum(jnp.maximum(drawn, -limit), limit).astype(held_as)


def setup_inputs(seed: int = 0) -> dict:
    seeds = jax.random.split(jax.random.key(seed), 8)
    return {
        "query": centred(seeds[0], (N_SECTION, MB, SEQ, HEADS * HD), 1.0, 6.0, ((0, 16), (2, 16))),
        "keys_values": centred(seeds[1], (N_SECTION, MB, 2, SEQ, KV_HEADS * HD), 1.0, 6.0, ((0, 16), (3, 16))),
        "grad_out": centred(seeds[2], (N_SECTION, MB, SEQ, HEADS * HD), 1.0, 6.0, ((0, 16), (2, 16))),
        "fwd_query": centred(seeds[3], (N_SECTION, MB, SEQ, HEADS * HD), 1.0, 6.0, ((0, 16), (2, 16))),
        "fwd_keys_values": centred(seeds[4], (N_SECTION, MB, 2, SEQ, KV_HEADS * HD), 1.0, 6.0, ((0, 16), (3, 16))),
        "held_out": centred(seeds[5], (N_SECTION, MB, SEQ, HEADS * HD), 0.25, 4.0, ((0, 16), (3, 16))),
        "evict": touch_ends(jax.random.randint(seeds[6], (N_SECTION // 2, 2, MB), 0, 2), jax.random.fold_in(seeds[6], 1), 0, 1).astype(jnp.int32),
    }


def attend(query, keys, values):
    scale = 1.0 / math.sqrt(HD)
    scores = jnp.dot(query, keys.T, preferred_element_type=jnp.float32) * scale
    rows = jnp.arange(SEQ)[:, None]
    cols = jnp.arange(SEQ)[None, :]
    scores = jnp.where(cols <= rows, scores, -jnp.inf)
    top = lax.optimization_barrier(jnp.max(scores, axis=1, keepdims=True))
    lse = top[:, 0] + jnp.log(lax.optimization_barrier(jnp.sum(jnp.exp(scores - top), axis=1)))
    prob = jnp.exp(scores - lse[:, None])
    prob_b = prob.astype(jnp.bfloat16)
    out_b = jnp.dot(prob_b, values, preferred_element_type=jnp.float32).astype(jnp.bfloat16)
    return (out_b, prob, prob_b)

def forward_head(query, keys, values):
    return attend(query, keys, values)[0]

def backward_head(query, keys, values, grad, held, flag):
    scale = 1.0 / math.sqrt(HD)
    out_b, prob, prob_b = attend(query, keys, values)
    used = lax.optimization_barrier(jnp.where(flag, held, out_b))
    dprob = jnp.dot(grad, values.T, preferred_element_type=jnp.float32)
    delta = lax.optimization_barrier(jnp.sum(grad.astype(jnp.float32) * used.astype(jnp.float32), axis=1))
    dscore = (prob * (dprob - delta[:, None])).astype(jnp.bfloat16)
    dquery = (jnp.dot(dscore, keys, preferred_element_type=jnp.float32) * scale).astype(jnp.bfloat16)
    dkeys = jnp.dot(dscore.T, query, preferred_element_type=jnp.float32) * scale
    dvalues = jnp.dot(prob_b.T, grad, preferred_element_type=jnp.float32)
    return (dquery, dkeys, dvalues)

def forward_group(item):
    queries, keys, values = item
    return jax.vmap(forward_head, in_axes=(0, None, None))(queries, keys, values)

def backward_group(item):
    queries, keys, values, grads, helds, flag = item
    dquery, dkeys, dvalues = jax.vmap(backward_head, in_axes=(0, None, None, 0, 0, None))(queries, keys, values, grads, helds, flag)
    return (dquery, lax.optimization_barrier(jnp.sum(dkeys, axis=0)), lax.optimization_barrier(jnp.sum(dvalues, axis=0)))

def head_items(array):
    group = HEADS // KV_HEADS
    count = N_SECTION * MB * KV_HEADS
    return array.reshape(N_SECTION, MB, SEQ, KV_HEADS, group, HD).transpose(0, 1, 3, 4, 2, 5).reshape(count, group, SEQ, HD)

def head_full(items):
    group = HEADS // KV_HEADS
    return items.reshape(N_SECTION, MB, KV_HEADS, group, SEQ, HD).transpose(0, 1, 4, 2, 3, 5).reshape(N_SECTION, MB, SEQ, HEADS * HD)

def kv_items(array):
    count = N_SECTION * MB * KV_HEADS
    return array.reshape(N_SECTION, MB, SEQ, KV_HEADS, HD).transpose(0, 1, 3, 2, 4).reshape(count, SEQ, HD)

def kv_full(items):
    return items.reshape(N_SECTION, MB, KV_HEADS, SEQ, HD).transpose(0, 1, 3, 2, 4).reshape(N_SECTION, MB, SEQ, KV_HEADS * HD)

def reference(query, keys_values, grad_out, fwd_query, fwd_keys_values, held_out, evict):
    count = N_SECTION * MB * KV_HEADS
    half = N_SECTION // 2
    fwd_items = lax.map(forward_group, (head_items(fwd_query), kv_items(fwd_keys_values[:, :, 0]), kv_items(fwd_keys_values[:, :, 1])))
    fwd_out = head_full(fwd_items)
    bwd_flags = jnp.concatenate([evict[:, 1], jnp.zeros_like(evict[:, 1])], axis=0) == 1
    flag_items = jnp.broadcast_to(bwd_flags[:, :, None], (N_SECTION, MB, KV_HEADS)).reshape(count)
    held_src = held_out[::-1]
    dquery, dkeys, dvalues = lax.map(backward_group, (head_items(query), kv_items(keys_values[:, :, 0]), kv_items(keys_values[:, :, 1]), head_items(grad_out), head_items(held_src), flag_items))
    dq_full = head_full(dquery)
    grad_kv = jnp.stack([kv_full(dkeys), kv_full(dvalues)], axis=2).astype(jnp.bfloat16)
    passed_on = jnp.concatenate([jnp.zeros_like(fwd_out[:1]), fwd_out[:-1]], axis=0)
    fwd_flags = jnp.concatenate([evict[:, 0], jnp.zeros_like(evict[:, 0])], axis=0) == 1
    marked_out = jnp.where(fwd_flags[:, :, None, None], fwd_out, jnp.zeros_like(fwd_out))
    mirror_out = jnp.concatenate([jnp.zeros_like(marked_out[:half]), marked_out[:half][::-1]], axis=0)
    return (passed_on, dq_full, grad_kv, mirror_out)
```

```python
import math

import jax
import jax.numpy as jnp
from jax import lax
from jax.experimental import pallas as pl
from jax.experimental.pallas import tpu as pltpu
from jax.sharding import PartitionSpec as P

HD = 128
NY = 4
NZ = 4
ROWS = 64
WIDE = 1024
SUPER = 256
SCALE = 1.0 / math.sqrt(HD)
LOG2E = math.log2(math.e)
F32 = jnp.float32
BF16 = jnp.bfloat16

VMEM = pl.BlockSpec(memory_space=pltpu.VMEM)
SMEM = pl.BlockSpec(memory_space=pltpu.SMEM)


def call(body, outs, scratch=(), flops=0, nbytes=1 << 20, exps=0):
    def run(meta, *args):
        return pl.pallas_call(
            body,
            out_shape=[jax.ShapeDtypeStruct(s, d) for s, d in outs],
            in_specs=[SMEM] + [VMEM] * len(args),
            out_specs=[VMEM] * len(outs),
            scratch_shapes=list(scratch),
            compiler_params=pltpu.CompilerParams(vmem_limit_bytes=48 * 1024 * 1024),
            cost_estimate=pl.CostEstimate(
                flops=flops, bytes_accessed=nbytes, transcendentals=exps
            ),
        )(meta, *args)

    return run


def at(index, size):
    return pl.ds(pl.multiple_of(index * size, size), size)


def pack_kv_body(meta, fkv, bkv, *outs):
    y = meta[0]
    for k in range(NY):
        to = (y + k) % NY
        outs[k][0] = fkv[:, :, :, at(to, HD)]
        outs[k][1] = bkv[:, :, :, at(to, HD)]


def pack_one_body(meta, x, *outs):
    y = meta[0]
    for k in range(NY):
        outs[k][...] = x[:, :, at((y + k) % NY, WIDE)]


def pack_two_body(meta, a, b, *outs):
    y = meta[0]
    for k in range(NY):
        to = (y + k) % NY
        outs[k][0] = a[:, :, at(to, WIDE)]
        outs[k][1] = b[:, :, at(to, WIDE)]


def pack_held_body(meta, held, *outs):
    z = meta[1]
    for k in range(NZ):
        to = z ^ k
        for m in range(2):
            for yy in range(NY):
                outs[k][m, yy] = held[m, pl.ds(pl.multiple_of(yy * SUPER + to * ROWS, ROWS), ROWS), :]


def join_kv_body(meta, b0, b1, b2, b3, fwd, bwd):
    y = meta[0]
    for k, block in enumerate((b0, b1, b2, b3)):
        source = (y + NY - k) % NY
        fwd[source] = block[0]
        bwd[source] = block[1]


def join_wide_body(meta, b0, b1, b2, b3, out):
    y = meta[0]
    for k, block in enumerate((b0, b1, b2, b3)):
        out[:, :, at((y + NY - k) % NY, WIDE)] = block[...]


def join_mirror_body(meta, b0, b1, b2, b3, out):
    z = meta[1]
    for k, block in enumerate((b0, b1, b2, b3)):
        source = z ^ k
        for m in range(2):
            for yy in range(NY):
                out[m, pl.ds(pl.multiple_of(yy * SUPER + source * ROWS, ROWS), ROWS), :] = block[m, yy]


def reduce_kv_body(meta, own, b1, b2, b3, *outs):
    y = meta[0]
    for k in range(NY):
        to = (y + k) % NY
        total = own[to] + b1[to].astype(F32)
        total = total + (b2[to].astype(F32) + b3[to].astype(F32))
        outs[k][...] = total.astype(BF16)


def join_grad_kv_body(meta, b0, b1, b2, b3, out):
    y = meta[0]
    for k, block in enumerate((b0, b1, b2, b3)):
        out[:, :, :, at((y + NY - k) % NY, HD)] = block[...]


def load_heads(scratch, blocks, y, pick):
    for k, block in enumerate(blocks):
        source = (y + NY - k) % NY
        for m in range(2):
            for h in range(8):
                rows = slice((h % 4) * ROWS, (h % 4 + 1) * ROWS)
                cols = slice(h * HD, (h + 1) * HD)
                scratch[source, m, h // 4, rows, :] = pick(block, m, cols)


def load_keys(keys, values, blocks, z):
    for k, block in enumerate(blocks):
        source = z ^ k
        for m in range(2):
            for yy in range(NY):
                rows = pl.ds(pl.multiple_of(yy * SUPER + source * ROWS, ROWS), ROWS)
                keys[m, rows, :] = block[yy, m, 0]
                values[m, rows, :] = block[yy, m, 1]


def transposed(x):
    return x.astype(F32).T.astype(BF16)


def dot_nt(a, b):
    return lax.dot_general(a, b, (((1,), (1,)), ((), ())), preferred_element_type=F32)


def dot_nn(a, b):
    return lax.dot_general(a, b, (((1,), (0,)), ((), ())), preferred_element_type=F32)


def seen(z):
    key = lax.broadcasted_iota(jnp.int32, (SUPER, SUPER), 0)
    row = lax.broadcasted_iota(jnp.int32, (SUPER, SUPER), 1) % ROWS + z * ROWS
    return key <= row


def score_blocks(keys, m, q, stripe, mask):
    blocks = []
    for j in range(stripe + 1):
        s = dot_nt(keys[m, j * SUPER : (j + 1) * SUPER, :], q)
        if j == stripe:
            s = jnp.where(mask, s, -jnp.inf)
        blocks.append(s)
    top = blocks[0].max(axis=0, keepdims=True)
    for s in blocks[1:]:
        top = jnp.maximum(top, s.max(axis=0, keepdims=True))
    shift = top * (SCALE * LOG2E)
    exps = [jnp.exp2(s * (SCALE * LOG2E) - shift) for s in blocks]
    total = exps[0].sum(axis=0, keepdims=True)
    for e in exps[1:]:
        total = total + e.sum(axis=0, keepdims=True)
    return exps, 1.0 / total


def forward_body(meta, q0, q1, q2, q3, k0, k1, k2, k3, *rest):
    passes, mirrors = rest[:4], rest[4:8]
    qs, keys, values, values_t, outs = rest[8:]
    y, z = meta[0], meta[1]
    load_heads(qs, (q0, q1, q2, q3), y, lambda b, m, c: b[m, :, c])
    load_keys(keys, values, (k0, k1, k2, k3), z)
    for m in range(2):
        values_t[m] = transposed(values[m])
    mask = seen(z)

    @pl.loop(0, 4)
    def _(t):
        m, half = t // 2, t % 2
        for stripe in range(NY):
            exps, inverse = score_blocks(keys, m, qs[stripe, m, half], stripe, mask)
            out = jnp.zeros((HD, SUPER), F32)
            for j, e in enumerate(exps):
                out += dot_nn(values_t[m, :, j * SUPER : (j + 1) * SUPER], e.astype(BF16))
            outs[stripe, m, half] = (out * inverse).T.astype(BF16)

    for k in range(NY):
        to = (y + k) % NY
        for m in range(2):
            for h in range(8):
                rows = slice((h % 4) * ROWS, (h % 4 + 1) * ROWS)
                passes[k][m, :, h * HD : (h + 1) * HD] = outs[to, m, h // 4, rows, :]
    for k in range(NZ):
        to = z ^ k
        for m in range(2):
            sent = meta[2 + m] == 1
            for yy in range(NY):
                for e in range(2):
                    rows = pl.ds(pl.multiple_of((to % 2) * 128 + e * ROWS, ROWS), ROWS)
                    piece = outs[yy, m, to // 2, rows, :]
                    mirrors[k][m, yy, :, e * HD : (e + 1) * HD] = jnp.where(
                        sent, piece, jnp.zeros_like(piece)
                    )


def backward_body(meta, *rest):
    qg, kv, held = rest[:4], rest[4:8], rest[8:12]
    dqs, dkvs = rest[12:16], rest[16:20]
    qs, gs, hs, keys, values, keys_t, outs, dkeys, dvalues = rest[20:]
    y, z = meta[0], meta[1]
    load_heads(qs, qg, y, lambda b, m, c: b[0, m, :, c])
    load_heads(gs, qg, y, lambda b, m, c: b[1, m, :, c])
    load_keys(keys, values, kv, z)
    for k, block in enumerate(held):
        source = z ^ k
        for m in range(2):
            for yy in range(NY):
                for e in range(2):
                    rows = pl.ds(pl.multiple_of((source % 2) * 128 + e * ROWS, ROWS), ROWS)
                    hs[yy, m, source // 2, rows, :] = block[m, yy, :, e * HD : (e + 1) * HD]
    for m in range(2):
        keys_t[m] = transposed(keys[m])
    dkeys[...] = jnp.zeros_like(dkeys)
    dvalues[...] = jnp.zeros_like(dvalues)
    mask = seen(z)

    @pl.loop(0, 4)
    def _(t):
        m, half = t // 2, t % 2
        marked = meta[4 + m] == 1
        for stripe in range(NY):
            q, g = qs[stripe, m, half], gs[stripe, m, half]
            exps, inverse = score_blocks(keys, m, q, stripe, mask)
            kept = (g.astype(F32) * hs[stripe, m, half].astype(F32)).T
            kept = kept.sum(axis=0, keepdims=True)
            probs, dprobs = [], []
            delta = jnp.zeros((1, SUPER), F32)
            for j, e in enumerate(exps):
                p = e * inverse
                dp = dot_nt(values[m, j * SUPER : (j + 1) * SUPER, :], g)
                delta += (p * dp).sum(axis=0, keepdims=True)
                probs.append(p)
                dprobs.append(dp)
            delta = jnp.where(marked, kept, delta)
            dq = jnp.zeros((HD, SUPER), F32)
            for j, (p, dp) in enumerate(zip(probs, dprobs)):
                rows = slice(j * SUPER, (j + 1) * SUPER)
                ds = (p * (dp - delta)).astype(BF16)
                dq += dot_nn(keys_t[m, :, rows], ds)
                dkeys[m, rows, :] += dot_nn(ds, q)
                dvalues[m, rows, :] += dot_nn(p.astype(BF16), g)
            outs[stripe, m, half] = (dq * SCALE).T.astype(BF16)

    for k in range(NY):
        to = (y + k) % NY
        for m in range(2):
            for h in range(8):
                rows = slice((h % 4) * ROWS, (h % 4 + 1) * ROWS)
                dqs[k][m, :, h * HD : (h + 1) * HD] = outs[to, m, h // 4, rows, :]
    for k in range(NZ):
        to = z ^ k
        for m in range(2):
            for yy in range(NY):
                rows = pl.ds(pl.multiple_of(yy * SUPER + to * ROWS, ROWS), ROWS)
                dkvs[k][yy, m, 0] = (dkeys[m, rows, :] * SCALE).astype(dkvs[k].dtype)
                dkvs[k][yy, m, 1] = dvalues[m, rows, :].astype(dkvs[k].dtype)


def per_device(query, keys_values, grad_out, fwd_query, fwd_keys_values, held_out, evict):
    sections = lax.axis_size("section")
    half = sections // 2
    section = lax.axis_index("section")
    tp = lax.axis_index("tp")
    y, z = tp // NZ, tp % NZ
    flags = lax.dynamic_index_in_dim(evict, jnp.minimum(section, half - 1), 0, keepdims=False)
    flags = jnp.where(section < half, flags, 0)
    meta = jnp.concatenate([jnp.stack([y, z]).astype(jnp.int32), flags.reshape(4).astype(jnp.int32)])
    both = ("section", "tp")

    def index(s, yy, zz):
        return (s * NY + yy) * NZ + zz

    def along_y(x, k):
        pairs = [(yy * NZ + zz, (yy + k) % NY * NZ + zz) for yy in range(NY) for zz in range(NZ)]
        return lax.ppermute(x, "tp", pairs)

    def along_z(x, k):
        pairs = [(yy * NZ + zz, yy * NZ + (zz ^ k)) for yy in range(NY) for zz in range(NZ)]
        return lax.ppermute(x, "tp", pairs)

    def to_mirror(x, k, senders):
        pairs = [
            (index(s, yy, zz), index(sections - 1 - s, yy, zz ^ k))
            for s in senders
            for yy in range(NY)
            for zz in range(NZ)
        ]
        return lax.ppermute(x, both, pairs)

    def to_next(x, k):
        pairs = [
            (index(s, yy, zz), index(s + 1, (yy + k) % NY, zz))
            for s in range(sections - 1)
            for yy in range(NY)
            for zz in range(NZ)
        ]
        return lax.ppermute(x, both, pairs)

    kv_piece = ((2, 2, 2, ROWS, HD), BF16)
    kv_stripe = ((NY, 2, 2, ROWS, HD), BF16)
    wide = ((2, ROWS, WIDE), BF16)
    two_wide = ((2, 2, ROWS, WIDE), BF16)
    pair_piece = ((2, NY, ROWS, 2 * HD), BF16)
    heads = pltpu.VMEM((NY, 2, 2, SUPER, HD), BF16)
    whole = pltpu.VMEM((2, NZ * SUPER, HD), BF16)
    whole_t = pltpu.VMEM((2, HD, NZ * SUPER), BF16)
    total = pltpu.VMEM((2, NZ * SUPER, HD), F32)

    kv = call(pack_kv_body, [kv_piece] * NY)(meta, fwd_keys_values[0], keys_values[0])
    kv = [kv[0]] + [along_y(kv[k], k) for k in range(1, NY)]
    fq = call(pack_one_body, [wide] * NY, nbytes=2 << 20)(meta, fwd_query[0])
    fq = [fq[0]] + [along_y(fq[k], k) for k in range(1, NY)]
    fwd_kv, bwd_kv = call(join_kv_body, [kv_stripe] * 2)(meta, *kv)
    fwd_kv = [fwd_kv] + [along_z(fwd_kv, k) for k in range(1, NZ)]
    held = call(pack_held_body, [pair_piece] * NZ, nbytes=2 << 20)(meta, held_out[0])
    held = [to_mirror(held[k], k, range(half, sections)) for k in range(NZ)]
    qg = call(pack_two_body, [two_wide] * NY, nbytes=4 << 20)(meta, query[0], grad_out[0])
    qg = [qg[0]] + [along_y(qg[k], k) for k in range(1, NY)]
    bwd_kv = [bwd_kv] + [along_z(bwd_kv, k) for k in range(1, NZ)]

    pairs_done = 20 * 2 * 512 * 256
    fwd = call(
        forward_body,
        [wide] * NY + [pair_piece] * NZ,
        [heads, whole, whole, whole_t, heads],
        flops=4 * pairs_done * HD,
        nbytes=4 << 20,
        exps=pairs_done,
    )(meta, *fq, *fwd_kv)
    passed = [to_next(fwd[k], k) for k in range(NY)]
    mirror = [to_mirror(fwd[NY + k], k, range(half)) for k in range(NZ)]

    bwd = call(
        backward_body,
        [wide] * NY + [((NY, 2, 2, ROWS, HD), F32)] + [kv_stripe] * (NZ - 1),
        [heads, heads, heads, whole, whole, whole_t, heads, total, total],
        flops=10 * pairs_done * HD,
        nbytes=8 << 20,
        exps=pairs_done,
    )(meta, *qg, *bwd_kv, *held)
    dkv = [bwd[NY]] + [along_z(bwd[NY + k], k) for k in range(1, NZ)]
    dq = [bwd[0]] + [along_y(bwd[k], k) for k in range(1, NY)]
    dkv = call(reduce_kv_body, [((2, 2, ROWS, HD), BF16)] * NY)(meta, *dkv)
    dkv = [dkv[0]] + [along_y(dkv[k], k) for k in range(1, NY)]

    full = ((2, ROWS, NY * WIDE), BF16)
    (dq,) = call(join_wide_body, [full])(meta, *dq)
    (dkv,) = call(join_grad_kv_body, [((2, 2, ROWS, NY * HD), BF16)])(meta, *dkv)
    (passed,) = call(join_wide_body, [full])(meta, *passed)
    (mirror,) = call(join_mirror_body, [((2, NZ * SUPER, 2 * HD), BF16)])(meta, *mirror)
    return (passed[None], dq[None], dkv[None], mirror[None])


def solution(mesh):
    return jax.shard_map(
        per_device,
        mesh=mesh,
        in_specs=(
            P("section", None, "tp", None),
            P("section", None, None, "tp", None),
            P("section", None, "tp", None),
            P("section", None, "tp", None),
            P("section", None, None, "tp", None),
            P("section", None, None, "tp"),
            P(),
        ),
        out_specs=(
            P("section", None, "tp", None),
            P("section", None, "tp", None),
            P("section", None, None, "tp", None),
            P("section", None, None, "tp"),
        ),
        check_vma=False,
    )
```

```python
import math

import jax
import jax.numpy as jnp
from jax import lax
from jax.experimental import pallas as pl
from jax.experimental.pallas import tpu as pltpu
from jax.sharding import PartitionSpec as P

HD = 128
NY = 4
NZ = 4
ROWS = 64
WIDE = 1024
SUPER = 256
SCALE = 1.0 / math.sqrt(HD)
LOG2E = math.log2(math.e)
F32 = jnp.float32
BF16 = jnp.bfloat16

VMEM = pl.BlockSpec(memory_space=pltpu.VMEM)
SMEM = pl.BlockSpec(memory_space=pltpu.SMEM)


def call(body, outs, scratch=(), flops=0, nbytes=1 << 20, exps=0):
    def run(meta, *args):
        return pl.pallas_call(
            body,
            out_shape=[jax.ShapeDtypeStruct(s, d) for s, d in outs],
            in_specs=[SMEM] + [VMEM] * len(args),
            out_specs=[VMEM] * len(outs),
            scratch_shapes=list(scratch),
            compiler_params=pltpu.CompilerParams(vmem_limit_bytes=48 * 1024 * 1024),
            cost_estimate=pl.CostEstimate(
                flops=flops, bytes_accessed=nbytes, transcendentals=exps
            ),
        )(meta, *args)

    return run


def at(index, size):
    return pl.ds(pl.multiple_of(index * size, size), size)


def pack_kv_body(meta, fkv, bkv, *outs):
    y = meta[0]
    for k in range(NY):
        to = (y + k) % NY
        outs[k][0] = fkv[:, :, :, at(to, HD)]
        outs[k][1] = bkv[:, :, :, at(to, HD)]


def pack_one_body(meta, x, *outs):
    y = meta[0]
    for k in range(NY):
        outs[k][...] = x[:, :, at((y + k) % NY, WIDE)]


def pack_two_body(meta, a, b, *outs):
    y = meta[0]
    for k in range(NY):
        to = (y + k) % NY
        outs[k][0] = a[:, :, at(to, WIDE)]
        outs[k][1] = b[:, :, at(to, WIDE)]


def pack_held_body(meta, held, *outs):
    z = meta[1]
    for k in range(NZ):
        to = z ^ k
        for m in range(2):
            for yy in range(NY):
                outs[k][m, yy] = held[m, pl.ds(pl.multiple_of(yy * SUPER + to * ROWS, ROWS), ROWS), :]


def join_kv_body(meta, b0, b1, b2, b3, fwd, bwd):
    y = meta[0]
    for k, block in enumerate((b0, b1, b2, b3)):
        source = (y + NY - k) % NY
        fwd[source] = block[0]
        bwd[source] = block[1]


def pair_kv_body(meta, own, other, out):
    z = meta[1]
    out[z % 2] = own[...]
    out[1 - z % 2] = other[...]


def join_wide_body(meta, b0, b1, b2, b3, out):
    y = meta[0]
    for k, block in enumerate((b0, b1, b2, b3)):
        out[:, :, at((y + NY - k) % NY, WIDE)] = block[...]


def join_mirror_body(meta, b0, b1, b2, b3, out):
    z = meta[1]
    for k, block in enumerate((b0, b1, b2, b3)):
        source = z ^ k
        for m in range(2):
            for yy in range(NY):
                out[m, pl.ds(pl.multiple_of(yy * SUPER + source * ROWS, ROWS), ROWS), :] = block[m, yy]


def reduce_kv_body(meta, own, b1, b2, b3, *outs):
    y = meta[0]
    for k in range(NY):
        to = (y + k) % NY
        total = own[to] + b1[to].astype(F32)
        total = total + (b2[to].astype(F32) + b3[to].astype(F32))
        outs[k][...] = total.astype(BF16)


def join_grad_kv_body(meta, b0, b1, b2, b3, out):
    y = meta[0]
    for k, block in enumerate((b0, b1, b2, b3)):
        out[:, :, :, at((y + NY - k) % NY, HD)] = block[...]


def load_heads(scratch, blocks, y, pick):
    for k, block in enumerate(blocks):
        source = (y + NY - k) % NY
        for m in range(2):
            for h in range(8):
                rows = slice((h % 4) * ROWS, (h % 4 + 1) * ROWS)
                cols = slice(h * HD, (h + 1) * HD)
                scratch[source, m, h // 4, rows, :] = pick(block, m, cols)


def load_keys(keys, values, near, far_middle, far_end, z):
    middle = jnp.logical_or(z == 1, z == 2)
    for e in range(2):
        for m in range(2):
            for yy in range(NY):
                rows = [
                    pl.ds(pl.multiple_of(yy * SUPER + (pair * 2 + e) * ROWS, ROWS), ROWS)
                    for pair in (z // 2, 1 - z // 2)
                ]
                for c, held in enumerate((keys, values)):
                    held[m, rows[0], :] = near[e, yy, m, c]
                    held[m, rows[1], :] = jnp.where(middle, far_middle[e, yy, m, c], far_end[e, yy, m, c])


def load_keys_direct(keys, values, blocks, z):
    for k, block in enumerate(blocks):
        source = z ^ k
        for m in range(2):
            for yy in range(NY):
                rows = pl.ds(pl.multiple_of(yy * SUPER + source * ROWS, ROWS), ROWS)
                keys[m, rows, :] = block[yy, m, 0]
                values[m, rows, :] = block[yy, m, 1]


def transposed(x):
    return x.astype(F32).T.astype(BF16)


def dot_nt(a, b):
    return lax.dot_general(a, b, (((1,), (1,)), ((), ())), preferred_element_type=F32)


def dot_nn(a, b):
    return lax.dot_general(a, b, (((1,), (0,)), ((), ())), preferred_element_type=F32)


def seen(z):
    key = lax.broadcasted_iota(jnp.int32, (SUPER, SUPER), 0)
    row = lax.broadcasted_iota(jnp.int32, (SUPER, SUPER), 1) % ROWS + z * ROWS
    return key <= row


def score_blocks(keys, m, q, stripe, mask):
    blocks = []
    for j in range(stripe + 1):
        s = dot_nt(keys[m, j * SUPER : (j + 1) * SUPER, :], q)
        if j == stripe:
            s = jnp.where(mask, s, -jnp.inf)
        blocks.append(s)
    top = blocks[0].max(axis=0, keepdims=True)
    for s in blocks[1:]:
        top = jnp.maximum(top, s.max(axis=0, keepdims=True))
    shift = top * (SCALE * LOG2E)
    exps = [jnp.exp2(s * (SCALE * LOG2E) - shift) for s in blocks]
    total = exps[0].sum(axis=0, keepdims=True)
    for e in exps[1:]:
        total = total + e.sum(axis=0, keepdims=True)
    return exps, 1.0 / total


def forward_body(meta, q0, q1, q2, q3, k0, k1, k2, k3, *rest):
    passes, mirrors = rest[:4], rest[4:8]
    qs, keys, values, values_t, outs = rest[8:]
    y, z = meta[0], meta[1]
    load_heads(qs, (q0, q1, q2, q3), y, lambda b, m, c: b[m, :, c])
    load_keys_direct(keys, values, (k0, k1, k2, k3), z)
    for m in range(2):
        values_t[m] = transposed(values[m])
    mask = seen(z)

    @pl.loop(0, 4)
    def _(t):
        m, half = t // 2, t % 2
        for stripe in range(NY):
            exps, inverse = score_blocks(keys, m, qs[stripe, m, half], stripe, mask)
            out = jnp.zeros((HD, SUPER), F32)
            for j, e in enumerate(exps):
                out += dot_nn(values_t[m, :, j * SUPER : (j + 1) * SUPER], e.astype(BF16))
            outs[stripe, m, half] = (out * inverse).T.astype(BF16)

    for k in range(NY):
        to = (y + k) % NY
        for m in range(2):
            for h in range(8):
                rows = slice((h % 4) * ROWS, (h % 4 + 1) * ROWS)
                passes[k][m, :, h * HD : (h + 1) * HD] = outs[to, m, h // 4, rows, :]
    for k in range(NZ):
        to = z ^ k
        for m in range(2):
            sent = meta[2 + m] == 1
            for yy in range(NY):
                for e in range(2):
                    rows = pl.ds(pl.multiple_of((to % 2) * 128 + e * ROWS, ROWS), ROWS)
                    piece = outs[yy, m, to // 2, rows, :]
                    mirrors[k][m, yy, :, e * HD : (e + 1) * HD] = jnp.where(
                        sent, piece, jnp.zeros_like(piece)
                    )


def backward_body(meta, *rest):
    qg, kv, held = rest[:4], rest[4:7], rest[7:11]
    dqs, dkvs = rest[11:15], rest[15:19]
    qs, gs, hs, keys, values, keys_t, outs, dkeys, dvalues = rest[19:]
    y, z = meta[0], meta[1]
    load_heads(qs, qg, y, lambda b, m, c: b[0, m, :, c])
    load_heads(gs, qg, y, lambda b, m, c: b[1, m, :, c])
    load_keys(keys, values, *kv, z)
    for k, block in enumerate(held):
        source = z ^ k
        for m in range(2):
            for yy in range(NY):
                for e in range(2):
                    rows = pl.ds(pl.multiple_of((source % 2) * 128 + e * ROWS, ROWS), ROWS)
                    hs[yy, m, source // 2, rows, :] = block[m, yy, :, e * HD : (e + 1) * HD]
    for m in range(2):
        keys_t[m] = transposed(keys[m])
    dkeys[...] = jnp.zeros_like(dkeys)
    dvalues[...] = jnp.zeros_like(dvalues)
    mask = seen(z)

    @pl.loop(0, 4)
    def _(t):
        m, half = t // 2, t % 2
        marked = meta[4 + m] == 1
        for stripe in range(NY):
            q, g = qs[stripe, m, half], gs[stripe, m, half]
            exps, inverse = score_blocks(keys, m, q, stripe, mask)
            kept = (g.astype(F32) * hs[stripe, m, half].astype(F32)).T
            kept = kept.sum(axis=0, keepdims=True)
            probs, dprobs = [], []
            delta = jnp.zeros((1, SUPER), F32)
            for j, e in enumerate(exps):
                p = e * inverse
                dp = dot_nt(values[m, j * SUPER : (j + 1) * SUPER, :], g)
                delta += (p * dp).sum(axis=0, keepdims=True)
                probs.append(p)
                dprobs.append(dp)
            delta = jnp.where(marked, kept, delta)
            dq = jnp.zeros((HD, SUPER), F32)
            for j, (p, dp) in enumerate(zip(probs, dprobs)):
                rows = slice(j * SUPER, (j + 1) * SUPER)
                ds = (p * (dp - delta)).astype(BF16)
                dq += dot_nn(keys_t[m, :, rows], ds)
                dkeys[m, rows, :] += dot_nn(ds, q)
                dvalues[m, rows, :] += dot_nn(p.astype(BF16), g)
            outs[stripe, m, half] = (dq * SCALE).T.astype(BF16)

    for k in range(NY):
        to = (y + k) % NY
        for m in range(2):
            for h in range(8):
                rows = slice((h % 4) * ROWS, (h % 4 + 1) * ROWS)
                dqs[k][m, :, h * HD : (h + 1) * HD] = outs[to, m, h // 4, rows, :]
    for k in range(NZ):
        to = z ^ k
        for m in range(2):
            for yy in range(NY):
                rows = pl.ds(pl.multiple_of(yy * SUPER + to * ROWS, ROWS), ROWS)
                dkvs[k][yy, m, 0] = (dkeys[m, rows, :] * SCALE).astype(dkvs[k].dtype)
                dkvs[k][yy, m, 1] = dvalues[m, rows, :].astype(dkvs[k].dtype)


def per_device(query, keys_values, grad_out, fwd_query, fwd_keys_values, held_out, evict):
    sections = lax.axis_size("section")
    half = sections // 2
    section = lax.axis_index("section")
    tp = lax.axis_index("tp")
    y, z = tp // NZ, tp % NZ
    flags = lax.dynamic_index_in_dim(evict, jnp.minimum(section, half - 1), 0, keepdims=False)
    flags = jnp.where(section < half, flags, 0)
    meta = jnp.concatenate([jnp.stack([y, z]).astype(jnp.int32), flags.reshape(4).astype(jnp.int32)])
    both = ("section", "tp")

    def index(s, yy, zz):
        return (s * NY + yy) * NZ + zz

    def along_y(x, k):
        pairs = [(yy * NZ + zz, (yy + k) % NY * NZ + zz) for yy in range(NY) for zz in range(NZ)]
        return lax.ppermute(x, "tp", pairs)

    def along_z(x, k):
        pairs = [(yy * NZ + zz, yy * NZ + (zz ^ k)) for yy in range(NY) for zz in range(NZ)]
        return lax.ppermute(x, "tp", pairs)

    def to_mirror(x, k, senders):
        pairs = [
            (index(s, yy, zz), index(sections - 1 - s, yy, zz ^ k))
            for s in senders
            for yy in range(NY)
            for zz in range(NZ)
        ]
        return lax.ppermute(x, both, pairs)

    def to_next(x, k):
        pairs = [
            (index(s, yy, zz), index(s + 1, (yy + k) % NY, zz))
            for s in range(sections - 1)
            for yy in range(NY)
            for zz in range(NZ)
        ]
        return lax.ppermute(x, both, pairs)

    def spread_z(x):
        swapped = along_z(x, 1)
        (near,) = call(pair_kv_body, [kv_pair])(meta, x, swapped)
        middle = [(yy * NZ + a, yy * NZ + b) for yy in range(NY) for a, b in ((1, 2), (2, 1))]
        far_middle = lax.ppermute(near, "tp", middle)
        ends = [(yy * NZ + a, yy * NZ + b) for yy in range(NY) for a, b in ((1, 0), (2, 3))]
        return [near, far_middle, lax.ppermute(far_middle, "tp", ends)]

    kv_pair = ((2, NY, 2, 2, ROWS, HD), BF16)
    kv_piece = ((2, 2, 2, ROWS, HD), BF16)
    kv_stripe = ((NY, 2, 2, ROWS, HD), BF16)
    wide = ((2, ROWS, WIDE), BF16)
    two_wide = ((2, 2, ROWS, WIDE), BF16)
    pair_piece = ((2, NY, ROWS, 2 * HD), BF16)
    heads = pltpu.VMEM((NY, 2, 2, SUPER, HD), BF16)
    whole = pltpu.VMEM((2, NZ * SUPER, HD), BF16)
    whole_t = pltpu.VMEM((2, HD, NZ * SUPER), BF16)
    total = pltpu.VMEM((2, NZ * SUPER, HD), F32)

    kv = call(pack_kv_body, [kv_piece] * NY)(meta, fwd_keys_values[0], keys_values[0])
    kv = [kv[0]] + [along_y(kv[k], k) for k in range(1, NY)]
    fq = call(pack_one_body, [wide] * NY, nbytes=2 << 20)(meta, fwd_query[0])
    fq = [fq[0]] + [along_y(fq[k], k) for k in range(1, NY)]
    fwd_kv, bwd_kv = call(join_kv_body, [kv_stripe] * 2)(meta, *kv)
    fwd_kv = [fwd_kv] + [along_z(fwd_kv, k) for k in range(1, NZ)]
    held = call(pack_held_body, [pair_piece] * NZ, nbytes=2 << 20)(meta, held_out[0])
    held = [to_mirror(held[k], k, range(half, sections)) for k in range(NZ)]
    qg = call(pack_two_body, [two_wide] * NY, nbytes=4 << 20)(meta, query[0], grad_out[0])
    qg = [qg[0]] + [along_y(qg[k], k) for k in range(1, NY)]
    bwd_kv = spread_z(bwd_kv)

    pairs_done = 20 * 2 * 512 * 256
    fwd = call(
        forward_body,
        [wide] * NY + [pair_piece] * NZ,
        [heads, whole, whole, whole_t, heads],
        flops=4 * pairs_done * HD,
        nbytes=4 << 20,
        exps=pairs_done,
    )(meta, *fq, *fwd_kv)
    passed = [to_next(fwd[k], k) for k in range(NY)]
    mirror = [to_mirror(fwd[NY + k], k, range(half)) for k in range(NZ)]

    bwd = call(
        backward_body,
        [wide] * NY + [((NY, 2, 2, ROWS, HD), F32)] + [kv_stripe] * (NZ - 1),
        [heads, heads, heads, whole, whole, whole_t, heads, total, total],
        flops=10 * pairs_done * HD,
        nbytes=8 << 20,
        exps=pairs_done,
    )(meta, *qg, *bwd_kv, *held)
    dkv = [bwd[NY]] + [along_z(bwd[NY + k], k) for k in range(1, NZ)]
    dq = [bwd[0]] + [along_y(bwd[k], k) for k in range(1, NY)]
    dkv = call(reduce_kv_body, [((2, 2, ROWS, HD), BF16)] * NY)(meta, *dkv)
    dkv = [dkv[0]] + [along_y(dkv[k], k) for k in range(1, NY)]

    full = ((2, ROWS, NY * WIDE), BF16)
    (dq,) = call(join_wide_body, [full])(meta, *dq)
    (dkv,) = call(join_grad_kv_body, [((2, 2, ROWS, NY * HD), BF16)])(meta, *dkv)
    (passed,) = call(join_wide_body, [full])(meta, *passed)
    (mirror,) = call(join_mirror_body, [((2, NZ * SUPER, 2 * HD), BF16)])(meta, *mirror)
    return (passed[None], dq[None], dkv[None], mirror[None])


def solution(mesh):
    return jax.shard_map(
        per_device,
        mesh=mesh,
        in_specs=(
            P("section", None, "tp", None),
            P("section", None, None, "tp", None),
            P("section", None, "tp", None),
            P("section", None, "tp", None),
            P("section", None, None, "tp", None),
            P("section", None, None, "tp"),
            P(),
        ),
        out_specs=(
            P("section", None, "tp", None),
            P("section", None, "tp", None),
            P("section", None, None, "tp", None),
            P("section", None, None, "tp"),
        ),
        check_vma=False,
    )
```
